32 devices in a mesh: rep: 2 (over y), grp: 4 (over z), img: 4 (over x, core).
Axes of the slice: x: 2, y: 2, z: 4, core: 2. Of those that a mesh axis runs over, the one named last changes fastest.
Arguments:
- patches: bfloat16 [4, 512, 2560], P('grp', 'rep'), parts along dimension 1, may hold values from -6 to 6
- embed_kernel: bfloat16 [4, 2560, 1024], P('grp', None, 'img'), may hold values from -0.125 to 0.125
- location_embed: bfloat16 [64, 1024], P(None, 'img'), may hold values from -3 to 3
- attn_in: bfloat16 [2, 1024, 3, 1024], P(None, 'grp', None, 'img'), may hold values from -0.25 to 0.25
- attn_out: bfloat16 [2, 1024, 1024], P(None, 'img', 'grp'), may hold values from -0.1875 to 0.1875
- ffn_up: bfloat16 [1024, 4096], P('grp', 'img'), may hold values from -0.1875 to 0.1875
- ffn_down: bfloat16 [4096, 1024], P('img', 'grp'), may hold values from -0.09375 to 0.09375
- head_kernel: bfloat16 [4, 1024, 2560], P('grp', None, 'img'), may hold values from -0.1875 to 0.1875
Outputs:
- recon: bfloat16 [4, 512, 2560], P('grp', 'rep', 'img'), parts along dimension 1
The draws below stay inside these ranges and needn't reach their ends.
There are 2 independent parts, one for each index of `rep`. The reference program is written for one: setup_inputs(seed, part) draws one part's arguments, and reference() takes and returns one part's arrays. A program takes and returns all parts, laid end to end along the dimension named above; an argument that names none is the same for every part. Nothing has to cross between parts.
All inputs are finite; a program needn't handle non-finite values.
Results may differ from the reference program's by a relative error of at most 0.02.
Values may be sent and summed in bfloat16 or wider, within the bound.
A program may use at most 64 MiB of HBM per device.

```python
import jax
import jax.numpy as jnp
from jax import lax

D = 1024
FF = 4096
P_SIZE = 2560
LOC = 64
IMGS = 4
HD = 64
GROUPS = 4
ROWS = 256


def draw_attn_in(key, part):
    key = jax.random.fold_in(key, 7)
    base = jax.random.normal(key, (2, D, 3, D), jnp.float32) * D ** (-0.5)
    return jnp.clip(base, -0.25, 0.25).astype(jnp.bfloat16)


def block_scale(rng, shape, split, least, largest):
    loudness = 1.0
    for axis_at, shards_of in split:
        steps = jax.random.uniform(jax.random.fold_in(jax.random.fold_in(rng, 6), axis_at), (shards_of,), jnp.float32, least / len(split), largest / len(split))
        loudness = loudness * jnp.repeat(jnp.exp(steps), shape[axis_at] // shards_of).reshape((-1,) + (1,) * (len(shape) - 1 - axis_at))
    return loudness


def gaussian(stream_key, shape, scale, reach, pieces=(), kind=jnp.bfloat16):
    result = jax.random.normal(stream_key, shape, jnp.float32) * scale
    if len(pieces) > 0:
        result = block_scale(stream_key, shape, pieces, -0.22, 0.18) * result
    return jnp.clip(result, min=-reach, max=reach).astype(kind)


def setup_inputs(seed: int = 0, part: int = 0) -> dict:
    key_list = jax.random.split(jax.random.key(seed), 9)
    part_splits = jax.random.split(jax.random.fold_in(key_list[8], part), 9)
    return {
        "patches": gaussian(part_splits[0], (GROUPS, ROWS, P_SIZE), 1.0, 6.0, ((0, 4),)),
        "embed_kernel": gaussian(key_list[1], (GROUPS, P_SIZE, D), P_SIZE ** -0.5, 0.125, ((0, 4), (2, 4))),
        "location_embed": gaussian(key_list[2], (LOC, D), 0.5, 3.0, ((1, 4),)),
        "attn_in": draw_attn_in(jax.random.fold_in(key_list[8], 71), part),
        "attn_out": gaussian(key_list[4], (2, D, D), D ** -0.5, 0.1875, ((1, 4), (2, 4))),
        "ffn_up": gaussian(key_list[5], (D, FF), D ** -0.5, 0.1875, ((0, 4), (1, 4))),
        "ffn_down": gaussian(key_list[6], (FF, D), FF ** -0.5, 0.09375, ((0, 4), (1, 4))),
        "head_kernel": gaussian(key_list[7], (GROUPS, D, P_SIZE), D ** -0.5, 0.1875, ((0, 4), (2, 4))),
    }


def norm_rows(stream):
    values = stream.astype(jnp.float32)
    center = values - lax.optimization_barrier(jnp.mean(values, axis=-1, keepdims=True))
    spread = lax.optimization_barrier(jnp.mean(center * center, axis=-1, keepdims=True))
    return (center * lax.rsqrt(spread + 1e-05)).astype(jnp.bfloat16)

def attend(query, keys, values, layout, form_scores, form_out):
    tokens, width = query.shape
    heads = width // HD
    shape = layout + (heads, HD)
    qq = query.reshape(shape).astype(jnp.float32)
    kk = keys.reshape(shape).astype(jnp.float32)
    vv = values.reshape(shape).astype(jnp.float32)
    scores = jnp.einsum(form_scores, qq, kk) * HD ** (-0.5)
    top = lax.optimization_barrier(jnp.max(scores, axis=-1, keepdims=True))
    expo = jnp.exp(scores - top)
    probs = (expo / lax.optimization_barrier(jnp.sum(expo, axis=-1, keepdims=True))).astype(jnp.bfloat16)
    mixed = jnp.einsum(form_out, probs.astype(jnp.float32), vv)
    return mixed.astype(jnp.bfloat16).reshape(tokens, width)

def reference(patches, embed_kernel, location_embed, attn_in, attn_out, ffn_up, ffn_down, head_kernel):

    def embed_one(pair):
        return jax.nn.gelu(jnp.dot(pair[0], pair[1], preferred_element_type=jnp.float32), approximate=False)
    hidden = lax.map(embed_one, (patches, embed_kernel))
    stream = (hidden.reshape(GROUPS, IMGS, LOC, D) + location_embed.astype(jnp.float32)).astype(jnp.bfloat16)
    stream = stream.reshape(GROUPS * ROWS, D)

    def block(stream, index, layout, form_scores, form_out):
        normed = norm_rows(stream)
        qkv = jnp.dot(normed, attn_in[index].reshape(D, 3 * D), preferred_element_type=jnp.float32)
        qkv = qkv.astype(jnp.bfloat16).reshape(-1, 3, D)
        mixed = attend(qkv[:, 0], qkv[:, 1], qkv[:, 2], layout, form_scores, form_out)
        branch = jnp.dot(mixed, attn_out[index], preferred_element_type=jnp.float32)
        return (stream.astype(jnp.float32) + branch).astype(jnp.bfloat16)
    stream = block(stream, 0, (GROUPS * IMGS, LOC), 'ilhe,imhe->ihlm', 'ihlm,imhe->ilhe')
    stream = block(stream, 1, (GROUPS, ROWS), 'gmhe,kmhe->mhgk', 'mhgk,kmhe->gmhe')
    normed = norm_rows(stream)
    inner = jax.nn.gelu(jnp.dot(normed, ffn_up, preferred_element_type=jnp.float32), approximate=False)
    inner = inner.astype(jnp.bfloat16)
    branch = jnp.dot(inner, ffn_down, preferred_element_type=jnp.float32)
    stream = (stream.astype(jnp.float32) + branch).astype(jnp.bfloat16)
    stream = stream.reshape(GROUPS, ROWS, D)

    def head_one(pair):
        return jnp.dot(pair[0], pair[1], preferred_element_type=jnp.float32).astype(jnp.bfloat16)
    return lax.map(head_one, (stream, head_kernel))
```

```python
import functools
import math

import jax
import jax.numpy as jnp
from jax import lax
from jax.experimental import pallas as pl
from jax.experimental.pallas import tpu as pltpu
from jax.sharding import PartitionSpec as P

HD = 64
MESH = pl.DeviceIdType.MESH


def norm_rows(stream):
    values = stream.astype(jnp.float32)
    center = values - jnp.mean(values, axis=-1, keepdims=True)
    spread = jnp.mean(center * center, axis=-1, keepdims=True)
    return (center * lax.rsqrt(spread + 1e-05)).astype(jnp.bfloat16)


def attend(query, keys, values, layout, form_scores, form_out):
    tokens, width = query.shape
    heads = width // HD
    shape = layout + (heads, HD)
    scores = jnp.einsum(
        form_scores, query.reshape(shape), keys.reshape(shape), preferred_element_type=jnp.float32
    )
    scores = scores * HD ** (-0.5)
    top = jnp.max(scores, axis=-1, keepdims=True)
    expo = jnp.exp(scores - top)
    probs = (expo / jnp.sum(expo, axis=-1, keepdims=True)).astype(jnp.bfloat16)
    mixed = jnp.einsum(form_out, probs, values.reshape(shape), preferred_element_type=jnp.float32)
    return mixed.astype(jnp.bfloat16).reshape(tokens, width)


def widen(stream):
    return lax.all_gather(stream, "img", axis=1, tiled=True)


def add_branch(stream, branch):
    total = lax.psum(branch.astype(jnp.bfloat16), "img").astype(jnp.float32)
    return (stream.astype(jnp.float32) + total).astype(jnp.bfloat16)


def block(stream, w_in, w_out, layout, form_scores, form_out):
    normed = norm_rows(stream)
    model_width, triple, local_width = w_in.shape
    qkv = jnp.dot(
        normed, w_in.reshape(model_width, triple * local_width), preferred_element_type=jnp.float32
    )
    qkv = qkv.astype(jnp.bfloat16).reshape(-1, triple, local_width)
    mixed = attend(qkv[:, 0], qkv[:, 1], qkv[:, 2], layout, form_scores, form_out)
    branch = jnp.dot(mixed, w_out, preferred_element_type=jnp.float32)
    return add_branch(stream, branch)


def feed_forward(stream, w_up, w_down):
    normed = norm_rows(stream)
    inner = jax.nn.gelu(
        jnp.dot(normed, w_up, preferred_element_type=jnp.float32), approximate=False
    )
    inner = inner.astype(jnp.bfloat16)
    branch = jnp.dot(inner, w_down, preferred_element_type=jnp.float32)
    return add_branch(stream, branch)


def local(patches, embed_kernel, location_embed, attn_in, attn_out, ffn_up, ffn_down, head_kernel):
    loc_count = location_embed.shape[0]
    rows = patches.shape[1]
    images = rows // loc_count
    groups = lax.axis_size("grp")
    per_group = rows // groups

    def fetch(index):
        return (
            lax.all_gather(attn_in[index], "grp", axis=0, tiled=True),
            lax.all_gather(attn_out[index], "grp", axis=1, tiled=True),
        )

    hidden = jax.nn.gelu(
        jnp.dot(patches[0], embed_kernel[0], preferred_element_type=jnp.float32), approximate=False
    )
    share = (hidden.reshape(images, loc_count, -1) + location_embed.astype(jnp.float32)).astype(
        jnp.bfloat16
    )
    share = share.reshape(rows, -1)
    stream = widen(share)
    width = stream.shape[1]
    w_in, w_out = fetch(0)
    stream = block(stream, w_in, w_out, (images, loc_count), "ilhe,imhe->ihlm", "ihlm,imhe->ilhe")
    placed = lax.all_to_all(
        stream.reshape(1, rows, width), "grp", split_axis=1, concat_axis=0, tiled=True
    )
    placed = placed.reshape(groups * per_group, width)
    w_in, w_out = fetch(1)
    placed = block(placed, w_in, w_out, (groups, per_group), "gmhe,kmhe->mhgk", "mhgk,kmhe->gmhe")
    w_up, w_down = (
        lax.all_gather(ffn_up, "grp", axis=0, tiled=True),
        lax.all_gather(ffn_down, "grp", axis=1, tiled=True),
    )
    placed = feed_forward(placed, w_up, w_down)
    returned = lax.all_to_all(
        placed.reshape(groups, per_group, width), "grp", split_axis=0, concat_axis=1, tiled=True
    )
    final = returned.reshape(rows, width)
    recon = jnp.dot(final, head_kernel[0], preferred_element_type=jnp.float32).astype(jnp.bfloat16)
    return recon[None]


def gelu_exact(x):
    return 0.5 * x * (1.0 + lax.erf(x * math.sqrt(0.5)))


def mm(a, b):
    return jnp.dot(a, b, preferred_element_type=jnp.float32)


def normalise(values):
    center = values - jnp.mean(values, axis=-1, keepdims=True)
    spread = jnp.mean(center * center, axis=-1, keepdims=True)
    return (center * lax.rsqrt(spread + 1e-05)).astype(jnp.bfloat16)


def head_attention(query, keys, values, mask):
    tokens, width = query.shape
    lane_head = lax.broadcasted_iota(jnp.int32, (tokens, width), 1) // HD
    mixed = jnp.zeros((tokens, width), jnp.float32)
    for head in range(width // HD):
        here = lane_head == head
        own = jnp.where(here, query, 0.0).astype(jnp.bfloat16)
        scores = lax.dot_general(
            own, keys, (((1,), (1,)), ((), ())), preferred_element_type=jnp.float32
        ) * HD ** (-0.5)
        scores = jnp.where(mask, scores, -jnp.inf)
        top = jnp.max(scores, axis=-1, keepdims=True)
        expo = jnp.exp(scores - top)
        probs = (expo / jnp.sum(expo, axis=-1, keepdims=True)).astype(jnp.bfloat16)
        mixed = jnp.where(here, mm(probs, values), mixed)
    return mixed.astype(jnp.bfloat16)


def fused(
    dims,
    patches, embed, loc_in, w_in0, w_in1, w_out, up, down, head,
    out,
    patches_v, embed_v, loc_v, head_v,
    win0, win1, wout0, wout1, up_v, down_v,
    feats, nrm0, nrm1, nrm2, part, rs, keep, a2a, back, fin, hid,
    zsend, zrecv, ysend, yrecv, xsend, xrecv, tsend, trecv, lsem, barrier_pad,
):
    n_rep, n_grp, n_img, rows, width = dims
    own = rows // n_img
    loc = own // n_grp
    y = lax.axis_index("rep")
    g = lax.axis_index("grp")
    i = lax.axis_index("img")

    def peer(me, n, d):
        return lax.rem(me + d, n)

    barrier = pltpu.get_barrier_semaphore()
    for axis, me, n in (("grp", g, n_grp), ("img", i, n_img), ("rep", y, n_rep)):
        for d in range(1, n):
            pl.semaphore_signal(
                barrier, inc=1, device_id={axis: peer(me, n, d)}, device_id_type=MESH
            )

    started = []

    def remote(src, dst, send, recv, axis, to):
        copy = pltpu.make_async_remote_copy(
            src_ref=src, dst_ref=dst, send_sem=send, recv_sem=recv,
            device_id={axis: to}, device_id_type=MESH,
        )
        copy.start()
        started.append(copy)

    def arrived(dst, send, recv, axis, to):
        pltpu.make_async_remote_copy(
            src_ref=dst, dst_ref=dst, send_sem=send, recv_sem=recv,
            device_id={axis: to}, device_id_type=MESH,
        ).wait_recv()

    def cut1(ref, half):
        size = ref.shape[0] // n_rep
        return ref.at[pl.ds(pl.multiple_of(half * size, size), size)]

    def cut2(ref, half):
        size = ref.shape[1] // n_rep
        return ref.at[:, pl.ds(pl.multiple_of(half * size, size), size)]

    weights = (
        (w_in0, win0, cut2),
        (w_out.at[0], wout0, cut1),
        (w_in1, win1, cut2),
        (w_out.at[1], wout1, cut1),
        (up, up_v, cut1),
        (down, down_v, cut1),
    )
    locals_ = []

    def local_copy(src, dst):
        copy = pltpu.make_async_copy(src, dst, lsem.at[len(locals_)])
        copy.start()
        locals_.append(copy)
        return copy

    def start_z(k):
        shard, full, cut = weights[k]
        for d in range(1, n_grp):
            remote(
                cut(shard, y), cut(full.at[g], y),
                zsend.at[k, d], zrecv.at[k, g], "grp", peer(g, n_grp, d),
            )

    def forward(k, hops=None):
        shard, full, cut = weights[k]
        for d in hops or range(1, n_grp):
            src = peer(g, n_grp, d)
            arrived(cut(full.at[src], y), zsend.at[k, d], zrecv.at[k, src], "grp", src)
            remote(
                cut(full.at[src], y), cut(full.at[src], y),
                ysend.at[k, d], yrecv.at[k, src], "rep", peer(y, n_rep, 1),
            )

    def ready(k):
        shard, full, cut = weights[k]
        for d in range(1, n_grp):
            src = peer(g, n_grp, d)
            half = peer(y, n_rep, 1)
            arrived(cut(full.at[src], half), ysend.at[k, d], yrecv.at[k, src], "rep", half)
        own_copies[k].wait()

    def spread(k, src_of, dst):
        for d in range(1, n_img):
            to = peer(i, n_img, d)
            remote(src_of(to), dst.at[i], xsend.at[k, d], xrecv.at[k, i], "img", to)

    def collected(k, dst):
        for d in range(1, n_img):
            src = peer(i, n_img, d)
            arrived(dst.at[src], xsend.at[k, d], xrecv.at[k, src], "img", src)

    in_copies = [
        local_copy(patches.at[0], patches_v),
        local_copy(embed.at[0], embed_v),
        local_copy(loc_in, loc_v),
    ]
    pl.semaphore_wait(barrier, n_grp + n_img + n_rep - 3)
    start_z(0)
    start_z(1)
    own_copies = [local_copy(shard, full.at[g]) for shard, full, cut in weights]
    head_copy = local_copy(head.at[0], head_v)

    for copy in in_copies:
        copy.wait()
    hidden = gelu_exact(mm(patches_v[...], embed_v[...]))
    places = loc_v[...].astype(jnp.float32)
    images = rows // places.shape[0]
    hidden = hidden.reshape(images, places.shape[0], hidden.shape[1]) + places[None]
    feats[i] = hidden.reshape(rows, hidden.shape[2]).astype(jnp.bfloat16)
    spread(0, lambda to: feats.at[i], feats)
    start_z(2)
    collected(0, feats)

    chunk = width // n_img
    chunks = [feats[s].astype(jnp.float32) for s in range(n_img)]
    mean = sum(jnp.sum(c, axis=-1, keepdims=True) for c in chunks) / width
    chunks = [c - mean for c in chunks]
    spread_ = sum(jnp.sum(c * c, axis=-1, keepdims=True) for c in chunks) / width
    scale = lax.rsqrt(spread_ + 1e-05)
    for s in range(n_img):
        nrm0[:, s * chunk:(s + 1) * chunk] = (chunks[s] * scale).astype(jnp.bfloat16)
    mine = pl.ds(pl.multiple_of(i * own, own), own)
    for s in range(n_img):
        keep[0, :, s * chunk:(s + 1) * chunk] = feats[s, mine, :]
    forward(0)
    start_z(3)
    forward(1)
    start_z(4)

    row_at = lax.broadcasted_iota(jnp.int32, (rows, rows), 0)
    col_at = lax.broadcasted_iota(jnp.int32, (rows, rows), 1)
    same_image = row_at // own == col_at // own
    same_place = jnp.logical_and(same_image, row_at % loc == col_at % loc)

    def project(normed, full):
        depth = width // n_grp
        total = None
        for s in range(n_grp):
            piece = normed[:, s * depth:(s + 1) * depth]
            terms = [mm(piece, full[s, p]) for p in range(3)]
            total = terms if total is None else [a + b for a, b in zip(total, terms)]
        return [t.astype(jnp.bfloat16) for t in total]

    def branch_out(k, mixed, full):
        wide = width // n_grp
        for s in range(n_grp):
            part[k, :, s * wide:(s + 1) * wide] = mm(mixed, full[s]).astype(jnp.bfloat16)
        spread(
            1 + 2 * k,
            lambda to: part.at[k, pl.ds(pl.multiple_of(to * own, own), own)],
            rs.at[k],
        )

    def summed(k, stream):
        total = part[k, mine, :].astype(jnp.float32)
        collected(1 + 2 * k, rs.at[k])
        for d in range(1, n_img):
            total = total + rs[k, peer(i, n_img, d)].astype(jnp.float32)
        return (stream.astype(jnp.float32) + total).astype(jnp.bfloat16)

    ready(0)
    query, keys, values = project(nrm0[...], win0)
    mixed = head_attention(query, keys, values, same_image)
    ready(1)
    branch_out(0, mixed, wout0)
    keep[1] = summed(0, keep[0])

    for d in range(1, n_grp):
        to = peer(g, n_grp, d)
        remote(
            keep.at[1, pl.ds(pl.multiple_of(to * loc, loc), loc)], a2a.at[g],
            tsend.at[0, d], trecv.at[0, g], "grp", to,
        )
    a2a[g] = keep[1, pl.ds(pl.multiple_of(g * loc, loc), loc), :]
    start_z(5)
    for d in range(1, n_grp):
        src = peer(g, n_grp, d)
        arrived(a2a.at[src], tsend.at[0, d], trecv.at[0, src], "grp", src)
    stream = a2a[...].reshape(own, width)
    nrm1[i] = normalise(stream.astype(jnp.float32))
    spread(2, lambda to: nrm1.at[i], nrm1)
    forward(2)
    forward(3)
    collected(2, nrm1)

    ready(2)
    query, keys, values = project(nrm1[...].reshape(rows, width), win1)
    mixed = head_attention(query, keys, values, same_place)
    ready(3)
    branch_out(1, mixed, wout1)
    stream = summed(1, stream)
    nrm2[i] = normalise(stream.astype(jnp.float32))
    spread(4, lambda to: nrm2.at[i], nrm2)
    forward(4)
    collected(4, nrm2)

    ready(4)
    normed = nrm2[...].reshape(rows, width)
    depth = width // n_grp
    total = None
    for s in range(n_grp):
        term = mm(normed[:, s * depth:(s + 1) * depth], up_v[s])
        total = term if total is None else total + term
    hid[...] = gelu_exact(total).astype(jnp.bfloat16)
    forward(5)
    ready(5)
    branch_out(2, hid[...], down_v)
    stream = summed(2, stream)

    back[...] = stream.reshape(n_grp, loc, width)
    fin[i, g] = back[g]
    for d in range(1, n_grp):
        to = peer(g, n_grp, d)
        remote(back.at[to], fin.at[i, g], tsend.at[1, d], trecv.at[1, g], "grp", to)
    for d in range(1, n_grp):
        src = peer(g, n_grp, d)
        arrived(fin.at[i, src], tsend.at[1, d], trecv.at[1, src], "grp", src)
    spread(6, lambda to: fin.at[i], fin)
    head_copy.wait()
    collected(6, fin)
    out[0] = mm(fin[...].reshape(rows, width), head_v[...]).astype(jnp.bfloat16)
    for copy in started:
        copy.wait_send()


def local_fused(mesh, patches, embed_kernel, location_embed, attn_in, attn_out, ffn_up, ffn_down, head_kernel):
    n_rep, n_grp, n_img = mesh.shape["rep"], mesh.shape["grp"], mesh.shape["img"]
    _, rows, p_size = patches.shape
    share = embed_kernel.shape[2]
    width = share * n_img
    loc_count = location_embed.shape[0]
    own = rows // n_img
    heads_w = attn_in.shape[3]
    depth = attn_in.shape[1]
    hidden = ffn_up.shape[1]
    recon_w = head_kernel.shape[2]
    place = own // n_grp
    w_in = attn_in.transpose(0, 2, 1, 3)
    bf = jnp.bfloat16
    dims = (n_rep, n_grp, n_img, rows, width)
    vm = lambda *s: pltpu.VMEM(s, bf)
    sem = lambda *s: pltpu.SemaphoreType.DMA(s)
    return pl.pallas_call(
        functools.partial(fused, dims),
        out_shape=jax.ShapeDtypeStruct((1, rows, recon_w), bf),
        in_specs=[pl.BlockSpec(memory_space=pl.ANY)] * 9,
        out_specs=pl.BlockSpec(memory_space=pltpu.VMEM),
        scratch_shapes=[
            vm(rows, p_size), vm(p_size, share), vm(loc_count, share), vm(width, recon_w),
            vm(n_grp, 3, depth, heads_w), vm(n_grp, 3, depth, heads_w),
            vm(n_grp, heads_w, depth), vm(n_grp, heads_w, depth),
            vm(n_grp, depth, hidden), vm(n_grp, hidden, depth),
            vm(n_img, rows, share), vm(rows, width), vm(n_img, own, width), vm(n_img, own, width),
            vm(3, rows, width), vm(3, n_img, own, width), vm(2, own, width),
            vm(n_grp, place, width), vm(n_grp, place, width), vm(n_img, n_grp, place, width),
            vm(rows, hidden),
            sem(6, n_grp), sem(6, n_grp), sem(6, n_grp), sem(6, n_grp),
            sem(7, n_img), sem(7, n_img), sem(2, n_grp), sem(2, n_grp),
            sem(10), pltpu.SemaphoreType.REGULAR,
        ],
        compiler_params=pltpu.CompilerParams(
            collective_id=0, has_side_effects=True, vmem_limit_bytes=48 * 1024 * 1024
        ),
    )(patches, embed_kernel, location_embed, w_in[0], w_in[1], attn_out, ffn_up, ffn_down, head_kernel)


def fits(mesh, rows):
    return mesh.shape["rep"] == 2 and rows % (mesh.shape["grp"] * mesh.shape["img"] * 16) == 0


def serve(mesh, patches, *weights):
    loc_count = weights[1].shape[0]
    rows = patches.shape[1]
    if fits(mesh, rows) and rows // loc_count == mesh.shape["img"]:
        return local_fused(mesh, patches, *weights)
    return local(patches, *weights)


def solution(mesh):
    return jax.shard_map(
        functools.partial(serve, mesh),
        mesh=mesh,
        in_specs=(
            P("grp", "rep", None),
            P("grp", None, "img"),
            P(None, "img"),
            P(None, "grp", None, "img"),
            P(None, "img", "grp"),
            P("grp", "img"),
            P("img", "grp"),
            P("grp", None, "img"),
        ),
        out_specs=P("grp", "rep", "img"),
        check_vma=False,
    )
```

```python
import functools
import math

import jax
import jax.numpy as jnp
from jax import lax
from jax.experimental import pallas as pl
from jax.experimental.pallas import tpu as pltpu
from jax.sharding import PartitionSpec as P

HD = 64
MESH = pl.DeviceIdType.MESH
SPLIT = (4, 1, 4, 1, 4, 4)
WINDOW = 3


def norm_rows(stream):
    values = stream.astype(jnp.float32)
    center = values - jnp.mean(values, axis=-1, keepdims=True)
    spread = jnp.mean(center * center, axis=-1, keepdims=True)
    return (center * lax.rsqrt(spread + 1e-05)).astype(jnp.bfloat16)


def attend(query, keys, values, layout, form_scores, form_out):
    tokens, width = query.shape
    heads = width // HD
    shape = layout + (heads, HD)
    scores = jnp.einsum(
        form_scores, query.reshape(shape), keys.reshape(shape), preferred_element_type=jnp.float32
    )
    scores = scores * HD ** (-0.5)
    top = jnp.max(scores, axis=-1, keepdims=True)
    expo = jnp.exp(scores - top)
    probs = (expo / jnp.sum(expo, axis=-1, keepdims=True)).astype(jnp.bfloat16)
    mixed = jnp.einsum(form_out, probs, values.reshape(shape), preferred_element_type=jnp.float32)
    return mixed.astype(jnp.bfloat16).reshape(tokens, width)


def widen(stream):
    return lax.all_gather(stream, "img", axis=1, tiled=True)


def add_branch(stream, branch):
    total = lax.psum(branch.astype(jnp.bfloat16), "img").astype(jnp.float32)
    return (stream.astype(jnp.float32) + total).astype(jnp.bfloat16)


def block(stream, w_in, w_out, layout, form_scores, form_out):
    normed = norm_rows(stream)
    model_width, triple, local_width = w_in.shape
    qkv = jnp.dot(
        normed, w_in.reshape(model_width, triple * local_width), preferred_element_type=jnp.float32
    )
    qkv = qkv.astype(jnp.bfloat16).reshape(-1, triple, local_width)
    mixed = attend(qkv[:, 0], qkv[:, 1], qkv[:, 2], layout, form_scores, form_out)
    branch = jnp.dot(mixed, w_out, preferred_element_type=jnp.float32)
    return add_branch(stream, branch)


def feed_forward(stream, w_up, w_down):
    normed = norm_rows(stream)
    inner = jax.nn.gelu(
        jnp.dot(normed, w_up, preferred_element_type=jnp.float32), approximate=False
    )
    inner = inner.astype(jnp.bfloat16)
    branch = jnp.dot(inner, w_down, preferred_element_type=jnp.float32)
    return add_branch(stream, branch)


def local(patches, embed_kernel, location_embed, attn_in, attn_out, ffn_up, ffn_down, head_kernel):
    loc_count = location_embed.shape[0]
    rows = patches.shape[1]
    images = rows // loc_count
    groups = lax.axis_size("grp")
    per_group = rows // groups

    def fetch(index):
        return (
            lax.all_gather(attn_in[index], "grp", axis=0, tiled=True),
            lax.all_gather(attn_out[index], "grp", axis=1, tiled=True),
        )

    hidden = jax.nn.gelu(
        jnp.dot(patches[0], embed_kernel[0], preferred_element_type=jnp.float32), approximate=False
    )
    share = (hidden.reshape(images, loc_count, -1) + location_embed.astype(jnp.float32)).astype(
        jnp.bfloat16
    )
    share = share.reshape(rows, -1)
    stream = widen(share)
    width = stream.shape[1]
    w_in, w_out = fetch(0)
    stream = block(stream, w_in, w_out, (images, loc_count), "ilhe,imhe->ihlm", "ihlm,imhe->ilhe")
    placed = lax.all_to_all(
        stream.reshape(1, rows, width), "grp", split_axis=1, concat_axis=0, tiled=True
    )
    placed = placed.reshape(groups * per_group, width)
    w_in, w_out = fetch(1)
    placed = block(placed, w_in, w_out, (groups, per_group), "gmhe,kmhe->mhgk", "mhgk,kmhe->gmhe")
    w_up, w_down = (
        lax.all_gather(ffn_up, "grp", axis=0, tiled=True),
        lax.all_gather(ffn_down, "grp", axis=1, tiled=True),
    )
    placed = feed_forward(placed, w_up, w_down)
    returned = lax.all_to_all(
        placed.reshape(groups, per_group, width), "grp", split_axis=0, concat_axis=1, tiled=True
    )
    final = returned.reshape(rows, width)
    recon = jnp.dot(final, head_kernel[0], preferred_element_type=jnp.float32).astype(jnp.bfloat16)
    return recon[None]


def gelu_exact(x):
    return 0.5 * x * (1.0 + lax.erf(x * math.sqrt(0.5)))


def mm(a, b):
    return jnp.dot(a, b, preferred_element_type=jnp.float32)


def normalise(values):
    center = values - jnp.mean(values, axis=-1, keepdims=True)
    spread = jnp.mean(center * center, axis=-1, keepdims=True)
    return (center * lax.rsqrt(spread + 1e-05)).astype(jnp.bfloat16)


def head_attention(query, keys, values, mask):
    tokens, width = query.shape
    lane_head = lax.broadcasted_iota(jnp.int32, (tokens, width), 1) // HD
    mixed = jnp.zeros((tokens, width), jnp.float32)
    for head in range(width // HD):
        here = lane_head == head
        own = jnp.where(here, query, 0.0).astype(jnp.bfloat16)
        scores = lax.dot_general(
            own, keys, (((1,), (1,)), ((), ())), preferred_element_type=jnp.float32
        ) * HD ** (-0.5)
        scores = jnp.where(mask, scores, -jnp.inf)
        top = jnp.max(scores, axis=-1, keepdims=True)
        expo = jnp.exp(scores - top)
        probs = (expo / jnp.sum(expo, axis=-1, keepdims=True)).astype(jnp.bfloat16)
        mixed = jnp.where(here, mm(probs, values), mixed)
    return mixed.astype(jnp.bfloat16)


def fused(
    dims,
    patches, embed, loc_in, w_in0, w_in1, w_out, up, down, head,
    out,
    patches_v, embed_v, loc_v, head_v,
    win0, win1, wout0, wout1, up_v, down_v,
    feats, nrm0, nrm1, nrm2, part, rs, keep, a2a, back, fin, hid,
    zsend, zrecv, ysend, yrecv, xsend, xrecv, tsend, trecv, lsem,
):
    n_rep, n_grp, n_img, rows, width = dims
    own = rows // n_img
    loc = own // n_grp
    y = lax.axis_index("rep")
    g = lax.axis_index("grp")
    i = lax.axis_index("img")

    def peer(me, n, d):
        return lax.rem(me + d, n)

    barrier = pltpu.get_barrier_semaphore()
    for axis, me, n in (("grp", g, n_grp), ("img", i, n_img), ("rep", y, n_rep)):
        for d in range(1, n):
            pl.semaphore_signal(
                barrier, inc=1, device_id={axis: peer(me, n, d)}, device_id_type=MESH
            )

    started, guarded = [], []

    def remote(src, dst, send, recv, axis, to):
        copy = pltpu.make_async_remote_copy(
            src_ref=src, dst_ref=dst, send_sem=send, recv_sem=recv,
            device_id={axis: to}, device_id_type=MESH,
        )
        copy.start()
        started.append(copy)

    def arrived(dst, send, recv, axis, to):
        pltpu.make_async_remote_copy(
            src_ref=dst, dst_ref=dst, send_sem=send, recv_sem=recv,
            device_id={axis: to}, device_id_type=MESH,
        ).wait_recv()

    tensors = ((w_in0, win0), (w_out.at[0], wout0), (w_in1, win1), (w_out.at[1], wout1), (up, up_v), (down, down_v))
    pieces = []
    for t, count in enumerate(SPLIT):
        pieces += [(t, count, at) for at in range(count)]

    def cut(t, count, at, ref, half):
        axis = 1 if t in (0, 2) else 0
        size = ref.shape[axis] // (n_rep * count)
        rows_at = pl.ds(pl.multiple_of((half * count + at) * size, size), size)
        return ref.at[:, rows_at] if axis else ref.at[rows_at]

    locals_ = []

    def local_copy(src, dst):
        copy = pltpu.make_async_copy(src, dst, lsem.at[len(locals_)])
        copy.start()
        locals_.append(copy)
        return copy

    last = n_grp - 1

    def remote_if(cond, src, dst, send, recv, to):
        copy = pltpu.make_async_remote_copy(
            src_ref=src, dst_ref=dst, send_sem=send, recv_sem=recv,
            device_id={"grp": to}, device_id_type=MESH,
        )
        pl.when(cond)(copy.start)
        guarded.append((cond, copy))

    def start_z(k):
        t, count, at = pieces[k]
        shard, full = tensors[t]
        for d in (2, -2, 1, -1):
            to = g + d
            inside = jnp.logical_and(to >= 0, to <= last)
            to = lax.min(lax.max(to, 0), last)
            remote_if(
                inside, cut(t, count, at, shard, y), cut(t, count, at, full.at[g], y),
                zsend.at[k, d + 2], zrecv.at[k, g], to,
            )

    def forward(k):
        if k + WINDOW < len(pieces):
            start_z(k + WINDOW)
        t, count, at = pieces[k]
        shard, full = tensors[t]
        inner = jnp.logical_and(g > 0, g < last)
        low = g < n_grp // 2
        order = (
            jnp.where(g == 0, 1, jnp.where(g == last, last - 1, jnp.where(low, 0, last))),
            jnp.where(g == 0, 2, jnp.where(g == last, last - 2, jnp.where(low, g + 1, g - 1))),
            jnp.where(g == 0, last, jnp.where(g == last, 0, jnp.where(low, last, 0))),
        )
        for n, src in enumerate(order):
            view = cut(t, count, at, full.at[src], y)
            arrived(view, zsend.at[k, 0], zrecv.at[k, src], "grp", src)
            if n == 2:
                outer = jnp.where(low, 0, last)
                away = jnp.where(outer == g, jnp.where(low, 1, last - 1), outer)
                remote_if(inner, view, view, zsend.at[k, 2], zrecv.at[k, src], away)
            remote(view, view, ysend.at[k, n], yrecv.at[k, src], "rep", peer(y, n_rep, 1))

    done = []

    def pump(t, share):
        upto = sum(SPLIT[:t]) + int(SPLIT[t] * share)
        while len(done) < upto:
            forward(len(done))
            done.append(1)

    def ready(t):
        half = peer(y, n_rep, 1)
        shard, full = tensors[t]
        for k, (of, count, at) in enumerate(pieces):
            if of == t:
                for d in range(1, n_grp):
                    src = peer(g, n_grp, d)
                    arrived(cut(t, count, at, full.at[src], half), ysend.at[k, d], yrecv.at[k, src], "rep", half)
        own_copies[t].wait()

    sibling = i + 1 - 2 * lax.rem(i, 2)
    across = lax.rem(i + 2, n_img)
    beyond = lax.rem(sibling + 2, n_img)

    def halves(ref):
        size = ref.shape[0] // 2
        return (ref.at[pl.ds(0, size)], ref.at[pl.ds(size, size)])

    def spread(k, dst):
        for h, view in enumerate(halves(dst.at[i])):
            remote(view, view, xsend.at[k, 0, h], xrecv.at[k, i, h], "img", across)
        for h, view in enumerate(halves(dst.at[i])):
            remote(view, view, xsend.at[k, 1, h], xrecv.at[k, i, h], "img", sibling)

    def collected(k, dst):
        for h, view in enumerate(halves(dst.at[across])):
            arrived(view, xsend.at[k, 0, h], xrecv.at[k, across, h], "img", across)
            remote(view, view, xsend.at[k, 2, h], xrecv.at[k, across, h], "img", sibling)
        for src in (sibling, beyond):
            for h, view in enumerate(halves(dst.at[src])):
                arrived(view, xsend.at[k, 1, h], xrecv.at[k, src, h], "img", sibling)

    in_copies = [
        local_copy(patches.at[0], patches_v),
        local_copy(embed.at[0], embed_v),
        local_copy(loc_in, loc_v),
    ]
    pl.semaphore_wait(barrier, n_grp + n_img + n_rep - 3)
    for k in range(WINDOW):
        start_z(k)
    own_copies = [local_copy(shard, full.at[g]) for shard, full in tensors]
    head_copy = local_copy(head.at[0], head_v)

    for copy in in_copies:
        copy.wait()
    hidden = gelu_exact(mm(patches_v[...], embed_v[...]))
    places = loc_v[...].astype(jnp.float32)
    images = rows // places.shape[0]
    hidden = hidden.reshape(images, places.shape[0], hidden.shape[1]) + places[None]
    feats[i] = hidden.reshape(rows, hidden.shape[2]).astype(jnp.bfloat16)
    spread(0, feats)
    collected(0, feats)

    chunk = width // n_img
    chunks = [feats[s].astype(jnp.float32) for s in range(n_img)]
    mean = sum(jnp.sum(c, axis=-1, keepdims=True) for c in chunks) / width
    chunks = [c - mean for c in chunks]
    spread_ = sum(jnp.sum(c * c, axis=-1, keepdims=True) for c in chunks) / width
    scale = lax.rsqrt(spread_ + 1e-05)
    for s in range(n_img):
        nrm0[:, s * chunk:(s + 1) * chunk] = (chunks[s] * scale).astype(jnp.bfloat16)
    mine = pl.ds(pl.multiple_of(i * own, own), own)
    for s in range(n_img):
        keep[0, :, s * chunk:(s + 1) * chunk] = feats[s, mine, :]

    pump(0, 1)

    row_at = lax.broadcasted_iota(jnp.int32, (rows, rows), 0)
    col_at = lax.broadcasted_iota(jnp.int32, (rows, rows), 1)
    same_image = row_at // own == col_at // own
    same_place = jnp.logical_and(same_image, row_at % loc == col_at % loc)

    def project(normed, full):
        depth = width // n_grp
        total = None
        for s in range(n_grp):
            piece = normed[:, s * depth:(s + 1) * depth]
            terms = [mm(piece, full[s, p]) for p in range(3)]
            total = terms if total is None else [a + b for a, b in zip(total, terms)]
        return [t.astype(jnp.bfloat16) for t in total]

    def branch_out(k, mixed, full):
        wide = width // n_grp
        for s in range(n_grp):
            part[k, :, s * wide:(s + 1) * wide] = mm(mixed, full[s]).astype(jnp.bfloat16)
        def rows_of(device):
            return pl.ds(pl.multiple_of(device * own, own), own)

        m = 1 + 2 * k
        for slot, to in ((0, beyond), (1, sibling)):
            remote(
                part.at[k, rows_of(to)], rs.at[k, slot],
                xsend.at[m, slot, 0], xrecv.at[m, slot, 0], "img", sibling,
            )
        arrived(rs.at[k, 0], xsend.at[m, 0, 0], xrecv.at[m, 0, 0], "img", sibling)
        pair = part[k, rows_of(across), :].astype(jnp.float32) + rs[k, 0].astype(jnp.float32)
        rs[k, 3] = pair.astype(jnp.bfloat16)
        remote(rs.at[k, 3], rs.at[k, 2], xsend.at[m, 2, 0], xrecv.at[m, 2, 0], "img", across)

    def summed(k, stream):
        m = 1 + 2 * k
        total = part[k, mine, :].astype(jnp.float32)
        for slot, src in ((1, sibling), (2, across)):
            arrived(rs.at[k, slot], xsend.at[m, slot, 0], xrecv.at[m, slot, 0], "img", src)
            total = total + rs[k, slot].astype(jnp.float32)
        return (stream.astype(jnp.float32) + total).astype(jnp.bfloat16)

    ready(0)
    query, keys, values = project(nrm0[...], win0)
    mixed = head_attention(query, keys, values, same_image)
    pump(1, 1)
    ready(1)
    branch_out(0, mixed, wout0)
    pump(2, 0.5)
    keep[1] = summed(0, keep[0])

    for d in range(1, n_grp):
        to = peer(g, n_grp, d)
        remote(
            keep.at[1, pl.ds(pl.multiple_of(to * loc, loc), loc)], a2a.at[g],
            tsend.at[0, d], trecv.at[0, g], "grp", to,
        )
    a2a[g] = keep[1, pl.ds(pl.multiple_of(g * loc, loc), loc), :]
    for d in range(1, n_grp):
        src = peer(g, n_grp, d)
        arrived(a2a.at[src], tsend.at[0, d], trecv.at[0, src], "grp", src)
    stream = a2a[...].reshape(own, width)
    nrm1[i] = normalise(stream.astype(jnp.float32))
    spread(2, nrm1)
    pump(2, 1)
    collected(2, nrm1)

    ready(2)
    query, keys, values = project(nrm1[...].reshape(rows, width), win1)
    pump(3, 1)
    mixed = head_attention(query, keys, values, same_place)
    ready(3)
    branch_out(1, mixed, wout1)
    pump(4, 0.5)
    stream = summed(1, stream)
    nrm2[i] = normalise(stream.astype(jnp.float32))
    spread(4, nrm2)
    pump(4, 1)
    collected(4, nrm2)

    ready(4)
    normed = nrm2[...].reshape(rows, width)
    depth = width // n_grp
    total = None
    for s in range(n_grp):
        term = mm(normed[:, s * depth:(s + 1) * depth], up_v[s])
        total = term if total is None else total + term
    hid[...] = gelu_exact(total).astype(jnp.bfloat16)
    pump(5, 1)
    ready(5)
    branch_out(2, hid[...], down_v)
    stream = summed(2, stream)

    back[...] = stream.reshape(n_grp, loc, width)
    fin[i, g] = back[g]
    for d in range(1, n_grp):
        to = peer(g, n_grp, d)
        remote(back.at[to], fin.at[i, g], tsend.at[1, d], trecv.at[1, g], "grp", to)
    for d in range(1, n_grp):
        src = peer(g, n_grp, d)
        arrived(fin.at[i, src], tsend.at[1, d], trecv.at[1, src], "grp", src)
    spread(6, fin)
    head_copy.wait()
    collected(6, fin)
    out[0] = mm(fin[...].reshape(rows, width), head_v[...]).astype(jnp.bfloat16)
    for copy in started:
        copy.wait_send()
    for cond, copy in guarded:
        pl.when(cond)(copy.wait_send)


def local_fused(mesh, patches, embed_kernel, location_embed, attn_in, attn_out, ffn_up, ffn_down, head_kernel):
    n_rep, n_grp, n_img = mesh.shape["rep"], mesh.shape["grp"], mesh.shape["img"]
    _, rows, p_size = patches.shape
    share = embed_kernel.shape[2]
    width = share * n_img
    loc_count = location_embed.shape[0]
    own = rows // n_img
    heads_w = attn_in.shape[3]
    depth = attn_in.shape[1]
    hidden = ffn_up.shape[1]
    recon_w = head_kernel.shape[2]
    place = own // n_grp
    w_in = attn_in.transpose(0, 2, 1, 3)
    bf = jnp.bfloat16
    dims = (n_rep, n_grp, n_img, rows, width)
    vm = lambda *s: pltpu.VMEM(s, bf)
    sem = lambda *s: pltpu.SemaphoreType.DMA(s)
    return pl.pallas_call(
        functools.partial(fused, dims),
        out_shape=jax.ShapeDtypeStruct((1, rows, recon_w), bf),
        in_specs=[pl.BlockSpec(memory_space=pl.ANY)] * 9,
        out_specs=pl.BlockSpec(memory_space=pltpu.VMEM),
        scratch_shapes=[
            vm(rows, p_size), vm(p_size, share), vm(loc_count, share), vm(width, recon_w),
            vm(n_grp, 3, depth, heads_w), vm(n_grp, 3, depth, heads_w),
            vm(n_grp, heads_w, depth), vm(n_grp, heads_w, depth),
            vm(n_grp, depth, hidden), vm(n_grp, hidden, depth),
            vm(n_img, rows, share), vm(rows, width), vm(n_img, own, width), vm(n_img, own, width),
            vm(3, rows, width), vm(3, n_img, own, width), vm(2, own, width),
            vm(n_grp, place, width), vm(n_grp, place, width), vm(n_img, n_grp, place, width),
            vm(rows, hidden),
            sem(sum(SPLIT), n_grp + 1), sem(sum(SPLIT), n_grp), sem(sum(SPLIT), n_grp), sem(sum(SPLIT), n_grp),
            sem(7, n_img, 2), sem(7, n_img, 2), sem(2, n_grp), sem(2, n_grp),
            sem(10),
        ],
        compiler_params=pltpu.CompilerParams(
            collective_id=0, has_side_effects=True, vmem_limit_bytes=60 * 1024 * 1024
        ),
    )(patches, embed_kernel, location_embed, w_in[0], w_in[1], attn_out, ffn_up, ffn_down, head_kernel)


def fits(mesh, rows):
    return mesh.shape["rep"] == 2 and mesh.shape["grp"] == 4 and mesh.shape["img"] == 4 and rows % (mesh.shape["grp"] * mesh.shape["img"] * 16) == 0


def serve(mesh, patches, *weights):
    loc_count = weights[1].shape[0]
    rows = patches.shape[1]
    if fits(mesh, rows) and rows // loc_count == mesh.shape["img"]:
        return local_fused(mesh, patches, *weights)
    return local(patches, *weights)


def solution(mesh):
    return jax.shard_map(
        functools.partial(serve, mesh),
        mesh=mesh,
        in_specs=(
            P("grp", "rep", None),
            P("grp", None, "img"),
            P(None, "img"),
            P(None, "grp", None, "img"),
            P(None, "img", "grp"),
            P("grp", "img"),
            P("img", "grp"),
            P("grp", None, "img"),
        ),
        out_specs=P("grp", "rep", "img"),
        check_vma=False,
    )
```

```python
import functools
import math

import jax
import jax.numpy as jnp
from jax import lax
from jax.experimental import pallas as pl
from jax.experimental.pallas import tpu as pltpu
from jax.sharding import PartitionSpec as P

HD = 64
MESH = pl.DeviceIdType.MESH
SPLIT = (4, 2, 4, 2, 4, 8)
WINDOW = 3


def norm_rows(stream):
    values = stream.astype(jnp.float32)
    center = values - jnp.mean(values, axis=-1, keepdims=True)
    spread = jnp.mean(center * center, axis=-1, keepdims=True)
    return (center * lax.rsqrt(spread + 1e-05)).astype(jnp.bfloat16)


def attend(query, keys, values, layout, form_scores, form_out):
    tokens, width = query.shape
    heads = width // HD
    shape = layout + (heads, HD)
    scores = jnp.einsum(
        form_scores, query.reshape(shape), keys.reshape(shape), preferred_element_type=jnp.float32
    )
    scores = scores * HD ** (-0.5)
    top = jnp.max(scores, axis=-1, keepdims=True)
    expo = jnp.exp(scores - top)
    probs = (expo / jnp.sum(expo, axis=-1, keepdims=True)).astype(jnp.bfloat16)
    mixed = jnp.einsum(form_out, probs, values.reshape(shape), preferred_element_type=jnp.float32)
    return mixed.astype(jnp.bfloat16).reshape(tokens, width)


def widen(stream):
    return lax.all_gather(stream, "img", axis=1, tiled=True)


def add_branch(stream, branch):
    total = lax.psum(branch.astype(jnp.bfloat16), "img").astype(jnp.float32)
    return (stream.astype(jnp.float32) + total).astype(jnp.bfloat16)


def block(stream, w_in, w_out, layout, form_scores, form_out):
    normed = norm_rows(stream)
    model_width, triple, local_width = w_in.shape
    qkv = jnp.dot(
        normed, w_in.reshape(model_width, triple * local_width), preferred_element_type=jnp.float32
    )
    qkv = qkv.astype(jnp.bfloat16).reshape(-1, triple, local_width)
    mixed = attend(qkv[:, 0], qkv[:, 1], qkv[:, 2], layout, form_scores, form_out)
    branch = jnp.dot(mixed, w_out, preferred_element_type=jnp.float32)
    return add_branch(stream, branch)


def feed_forward(stream, w_up, w_down):
    normed = norm_rows(stream)
    inner = jax.nn.gelu(
        jnp.dot(normed, w_up, preferred_element_type=jnp.float32), approximate=False
    )
    inner = inner.astype(jnp.bfloat16)
    branch = jnp.dot(inner, w_down, preferred_element_type=jnp.float32)
    return add_branch(stream, branch)


def local(patches, embed_kernel, location_embed, attn_in, attn_out, ffn_up, ffn_down, head_kernel):
    loc_count = location_embed.shape[0]
    rows = patches.shape[1]
    images = rows // loc_count
    groups = lax.axis_size("grp")
    per_group = rows // groups

    def fetch(index):
        return (
            lax.all_gather(attn_in[index], "grp", axis=0, tiled=True),
            lax.all_gather(attn_out[index], "grp", axis=1, tiled=True),
        )

    hidden = jax.nn.gelu(
        jnp.dot(patches[0], embed_kernel[0], preferred_element_type=jnp.float32), approximate=False
    )
    share = (hidden.reshape(images, loc_count, -1) + location_embed.astype(jnp.float32)).astype(
        jnp.bfloat16
    )
    share = share.reshape(rows, -1)
    stream = widen(share)
    width = stream.shape[1]
    w_in, w_out = fetch(0)
    stream = block(stream, w_in, w_out, (images, loc_count), "ilhe,imhe->ihlm", "ihlm,imhe->ilhe")
    placed = lax.all_to_all(
        stream.reshape(1, rows, width), "grp", split_axis=1, concat_axis=0, tiled=True
    )
    placed = placed.reshape(groups * per_group, width)
    w_in, w_out = fetch(1)
    placed = block(placed, w_in, w_out, (groups, per_group), "gmhe,kmhe->mhgk", "mhgk,kmhe->gmhe")
    w_up, w_down = (
        lax.all_gather(ffn_up, "grp", axis=0, tiled=True),
        lax.all_gather(ffn_down, "grp", axis=1, tiled=True),
    )
    placed = feed_forward(placed, w_up, w_down)
    returned = lax.all_to_all(
        placed.reshape(groups, per_group, width), "grp", split_axis=0, concat_axis=1, tiled=True
    )
    final = returned.reshape(rows, width)
    recon = jnp.dot(final, head_kernel[0], preferred_element_type=jnp.float32).astype(jnp.bfloat16)
    return recon[None]


def gelu_exact(x):
    return 0.5 * x * (1.0 + lax.erf(x * math.sqrt(0.5)))


def mm(a, b):
    return jnp.dot(a, b, preferred_element_type=jnp.float32)


def normalise(values):
    center = values - jnp.mean(values, axis=-1, keepdims=True)
    spread = jnp.mean(center * center, axis=-1, keepdims=True)
    return (center * lax.rsqrt(spread + 1e-05)).astype(jnp.bfloat16)


def head_attention(query, keys, values, mask):
    tokens, width = query.shape
    lane_head = lax.broadcasted_iota(jnp.int32, (tokens, width), 1) // HD
    mixed = jnp.zeros((tokens, width), jnp.float32)
    for head in range(width // HD):
        here = lane_head == head
        own = jnp.where(here, query, 0.0).astype(jnp.bfloat16)
        scores = lax.dot_general(
            own, keys, (((1,), (1,)), ((), ())), preferred_element_type=jnp.float32
        ) * HD ** (-0.5)
        scores = jnp.where(mask, scores, -jnp.inf)
        top = jnp.max(scores, axis=-1, keepdims=True)
        expo = jnp.exp(scores - top)
        probs = (expo / jnp.sum(expo, axis=-1, keepdims=True)).astype(jnp.bfloat16)
        mixed = jnp.where(here, mm(probs, values), mixed)
    return mixed.astype(jnp.bfloat16)


def fused(
    dims,
    patches, embed, loc_in, w_in0, w_in1, w_out, up, down, head,
    out,
    patches_v, embed_v, loc_v, head_v,
    win0, win1, wout0, wout1, up_v, down_v,
    feats, nrm0, nrm1, nrm2, part, rs, keep, a2a, back, fin, hid,
    zsend, zrecv, ysend, yrecv, xsend, xrecv, tsend, trecv, lsem,
):
    n_rep, n_grp, n_img, rows, width = dims
    own = rows // n_img
    loc = own // n_grp
    y = lax.axis_index("rep")
    g = lax.axis_index("grp")
    i = lax.axis_index("img")

    def peer(me, n, d):
        return lax.rem(me + d, n)

    barrier = pltpu.get_barrier_semaphore()
    for axis, me, n in (("grp", g, n_grp), ("img", i, n_img), ("rep", y, n_rep)):
        for d in range(1, n):
            pl.semaphore_signal(
                barrier, inc=1, device_id={axis: peer(me, n, d)}, device_id_type=MESH
            )

    started, guarded = [], []

    def remote(src, dst, send, recv, axis, to):
        copy = pltpu.make_async_remote_copy(
            src_ref=src, dst_ref=dst, send_sem=send, recv_sem=recv,
            device_id={axis: to}, device_id_type=MESH,
        )
        copy.start()
        started.append(copy)

    def arrived(dst, send, recv, axis, to):
        pltpu.make_async_remote_copy(
            src_ref=dst, dst_ref=dst, send_sem=send, recv_sem=recv,
            device_id={axis: to}, device_id_type=MESH,
        ).wait_recv()

    tensors = ((w_in0, win0), (w_out.at[0], wout0), (w_in1, win1), (w_out.at[1], wout1), (up, up_v), (down, down_v))
    pieces = []
    for t, count in enumerate(SPLIT):
        pieces += [(t, count, at) for at in range(count)]

    def cut(t, count, at, ref, half):
        axis = 1 if t in (0, 2) else 0
        size = ref.shape[axis] // (n_rep * count)
        rows_at = pl.ds(pl.multiple_of((half * count + at) * size, size), size)
        return ref.at[:, rows_at] if axis else ref.at[rows_at]

    locals_ = []

    def local_copy(src, dst):
        copy = pltpu.make_async_copy(src, dst, lsem.at[len(locals_)])
        copy.start()
        locals_.append(copy)
        return copy

    last = n_grp - 1

    def remote_if(cond, src, dst, send, recv, to):
        copy = pltpu.make_async_remote_copy(
            src_ref=src, dst_ref=dst, send_sem=send, recv_sem=recv,
            device_id={"grp": to}, device_id_type=MESH,
        )
        pl.when(cond)(copy.start)
        guarded.append((cond, copy))

    def start_z(k):
        t, count, at = pieces[k]
        shard, full = tensors[t]
        for d in (2, -2, 1, -1):
            to = g + d
            inside = jnp.logical_and(to >= 0, to <= last)
            to = lax.min(lax.max(to, 0), last)
            remote_if(
                inside, cut(t, count, at, shard, y), cut(t, count, at, full.at[g], y),
                zsend.at[k, d + 2], zrecv.at[k, g], to,
            )

    def forward(k, hops=(0, 1, 2)):
        if 0 in hops and k + WINDOW < len(pieces):
            start_z(k + WINDOW)
        t, count, at = pieces[k]
        shard, full = tensors[t]
        inner = jnp.logical_and(g > 0, g < last)
        low = g < n_grp // 2
        far = jnp.where(low, last, 0)
        order = (
            jnp.where(g == 0, 1, jnp.where(g == last, last - 1, far)),
            jnp.where(g == 0, 2, jnp.where(g == last, last - 2, jnp.where(low, g + 1, g - 1))),
            jnp.where(inner, jnp.where(low, 0, last), far),
        )
        for n in hops:
            src = order[n]
            view = cut(t, count, at, full.at[src], y)
            arrived(view, zsend.at[k, 0], zrecv.at[k, src], "grp", src)
            if n == 0:
                outer = jnp.where(low, 0, last)
                away = jnp.where(outer == g, jnp.where(low, 1, last - 1), outer)
                remote_if(inner, view, view, zsend.at[k, 2], zrecv.at[k, src], away)
            remote(view, view, ysend.at[k, n], yrecv.at[k, src], "rep", peer(y, n_rep, 1))

    done, late = [], [0]

    def pump(t, share):
        upto = sum(SPLIT[:t]) + int(SPLIT[t] * share)
        while len(done) < upto:
            forward(len(done), (0, 1))
            if len(done) > late[0]:
                forward(late[0], (2,))
                late[0] += 1
            done.append(1)
        if share == 1 and late[0] < len(done):
            forward(late[0], (2,))
            late[0] += 1

    def ready(t):
        half = peer(y, n_rep, 1)
        shard, full = tensors[t]
        for k, (of, count, at) in enumerate(pieces):
            if of == t:
                for d in range(1, n_grp):
                    src = peer(g, n_grp, d)
                    arrived(cut(t, count, at, full.at[src], half), ysend.at[k, d], yrecv.at[k, src], "rep", half)
        own_copies[t].wait()

    sibling = i + 1 - 2 * lax.rem(i, 2)
    across = lax.rem(i + 2, n_img)
    beyond = lax.rem(sibling + 2, n_img)

    def halves(ref):
        size = ref.shape[0] // 2
        return (ref.at[pl.ds(0, size)], ref.at[pl.ds(size, size)])

    def spread(k, dst):
        for h, view in enumerate(halves(dst.at[i])):
            remote(view, view, xsend.at[k, 0, h], xrecv.at[k, i, h], "img", across)
        for h, view in enumerate(halves(dst.at[i])):
            remote(view, view, xsend.at[k, 1, h], xrecv.at[k, i, h], "img", sibling)

    def collected(k, dst):
        for h, view in enumerate(halves(dst.at[across])):
            arrived(view, xsend.at[k, 0, h], xrecv.at[k, across, h], "img", across)
            remote(view, view, xsend.at[k, 2, h], xrecv.at[k, across, h], "img", sibling)
        for src in (sibling, beyond):
            for h, view in enumerate(halves(dst.at[src])):
                arrived(view, xsend.at[k, 1, h], xrecv.at[k, src, h], "img", sibling)

    in_copies = [
        local_copy(patches.at[0], patches_v),
        local_copy(embed.at[0], embed_v),
        local_copy(loc_in, loc_v),
    ]
    pl.semaphore_wait(barrier, n_grp + n_img + n_rep - 3)
    for k in range(WINDOW):
        start_z(k)
    own_copies = [local_copy(shard, full.at[g]) for shard, full in tensors]
    head_copy = local_copy(head.at[0], head_v)

    for copy in in_copies:
        copy.wait()
    hidden = gelu_exact(mm(patches_v[...], embed_v[...]))
    places = loc_v[...].astype(jnp.float32)
    images = rows // places.shape[0]
    hidden = hidden.reshape(images, places.shape[0], hidden.shape[1]) + places[None]
    feats[i] = hidden.reshape(rows, hidden.shape[2]).astype(jnp.bfloat16)
    spread(0, feats)
    collected(0, feats)

    chunk = width // n_img
    chunks = [feats[s].astype(jnp.float32) for s in range(n_img)]
    mean = sum(jnp.sum(c, axis=-1, keepdims=True) for c in chunks) / width
    chunks = [c - mean for c in chunks]
    spread_ = sum(jnp.sum(c * c, axis=-1, keepdims=True) for c in chunks) / width
    scale = lax.rsqrt(spread_ + 1e-05)
    for s in range(n_img):
        nrm0[:, s * chunk:(s + 1) * chunk] = (chunks[s] * scale).astype(jnp.bfloat16)
    mine = pl.ds(pl.multiple_of(i * own, own), own)
    for s in range(n_img):
        keep[0, :, s * chunk:(s + 1) * chunk] = feats[s, mine, :]

    pump(0, 1)

    row_at = lax.broadcasted_iota(jnp.int32, (rows, rows), 0)
    col_at = lax.broadcasted_iota(jnp.int32, (rows, rows), 1)
    same_image = row_at // own == col_at // own
    same_place = jnp.logical_and(same_image, row_at % loc == col_at % loc)

    def project(normed, full):
        depth = width // n_grp
        total = None
        for s in range(n_grp):
            piece = normed[:, s * depth:(s + 1) * depth]
            terms = [mm(piece, full[s, p]) for p in range(3)]
            total = terms if total is None else [a + b for a, b in zip(total, terms)]
        return [t.astype(jnp.bfloat16) for t in total]

    def branch_out(k, mixed, full):
        wide = width // n_grp
        for s in range(n_grp):
            part[k, :, s * wide:(s + 1) * wide] = mm(mixed, full[s]).astype(jnp.bfloat16)
        def rows_of(device):
            return pl.ds(pl.multiple_of(device * own, own), own)

        m = 1 + 2 * k
        for slot, to in ((0, beyond), (1, sibling)):
            remote(
                part.at[k, rows_of(to)], rs.at[k, slot],
                xsend.at[m, slot, 0], xrecv.at[m, slot, 0], "img", sibling,
            )
        arrived(rs.at[k, 0], xsend.at[m, 0, 0], xrecv.at[m, 0, 0], "img", sibling)
        pair = part[k, rows_of(across), :].astype(jnp.float32) + rs[k, 0].astype(jnp.float32)
        rs[k, 3] = pair.astype(jnp.bfloat16)
        remote(rs.at[k, 3], rs.at[k, 2], xsend.at[m, 2, 0], xrecv.at[m, 2, 0], "img", across)

    def summed(k, stream):
        m = 1 + 2 * k
        total = part[k, mine, :].astype(jnp.float32)
        for slot, src in ((1, sibling), (2, across)):
            arrived(rs.at[k, slot], xsend.at[m, slot, 0], xrecv.at[m, slot, 0], "img", src)
            total = total + rs[k, slot].astype(jnp.float32)
        return (stream.astype(jnp.float32) + total).astype(jnp.bfloat16)

    ready(0)
    query, keys, values = project(nrm0[...], win0)
    mixed = head_attention(query, keys, values, same_image)
    pump(1, 1)
    ready(1)
    branch_out(0, mixed, wout0)
    pump(2, 0.25)
    keep[1] = summed(0, keep[0])

    for d in range(1, n_grp):
        to = peer(g, n_grp, d)
        remote(
            keep.at[1, pl.ds(pl.multiple_of(to * loc, loc), loc)], a2a.at[g],
            tsend.at[0, d], trecv.at[0, g], "grp", to,
        )
    pump(2, 0.5)
    a2a[g] = keep[1, pl.ds(pl.multiple_of(g * loc, loc), loc), :]
    for d in range(1, n_grp):
        src = peer(g, n_grp, d)
        arrived(a2a.at[src], tsend.at[0, d], trecv.at[0, src], "grp", src)
    stream = a2a[...].reshape(own, width)
    nrm1[i] = normalise(stream.astype(jnp.float32))
    spread(2, nrm1)
    pump(2, 1)
    collected(2, nrm1)
    pump(3, 1)

    ready(2)
    query, keys, values = project(nrm1[...].reshape(rows, width), win1)
    pump(3, 1)
    mixed = head_attention(query, keys, values, same_place)
    ready(3)
    branch_out(1, mixed, wout1)
    pump(4, 0.25)
    stream = summed(1, stream)
    pump(4, 0.5)
    nrm2[i] = normalise(stream.astype(jnp.float32))
    spread(4, nrm2)
    pump(4, 1)
    pump(5, 0.125)
    collected(4, nrm2)
    pump(5, 0.25)

    ready(4)
    normed = nrm2[...].reshape(rows, width)
    depth = width // n_grp
    total = None
    for s in range(n_grp):
        term = mm(normed[:, s * depth:(s + 1) * depth], up_v[s])
        total = term if total is None else total + term
    hid[...] = gelu_exact(total).astype(jnp.bfloat16)
    pump(5, 1)
    ready(5)
    branch_out(2, hid[...], down_v)
    stream = summed(2, stream)

    back[...] = stream.reshape(n_grp, loc, width)
    fin[i, g] = back[g]
    for d in range(1, n_grp):
        to = peer(g, n_grp, d)
        remote(back.at[to], fin.at[i, g], tsend.at[1, d], trecv.at[1, g], "grp", to)
    for d in range(1, n_grp):
        src = peer(g, n_grp, d)
        arrived(fin.at[i, src], tsend.at[1, d], trecv.at[1, src], "grp", src)
    spread(6, fin)
    head_copy.wait()
    collected(6, fin)
    out[0] = mm(fin[...].reshape(rows, width), head_v[...]).astype(jnp.bfloat16)
    for copy in started:
        copy.wait_send()
    for cond, copy in guarded:
        pl.when(cond)(copy.wait_send)


def local_fused(mesh, patches, embed_kernel, location_embed, attn_in, attn_out, ffn_up, ffn_down, head_kernel):
    n_rep, n_grp, n_img = mesh.shape["rep"], mesh.shape["grp"], mesh.shape["img"]
    _, rows, p_size = patches.shape
    share = embed_kernel.shape[2]
    width = share * n_img
    loc_count = location_embed.shape[0]
    own = rows // n_img
    heads_w = attn_in.shape[3]
    depth = attn_in.shape[1]
    hidden = ffn_up.shape[1]
    recon_w = head_kernel.shape[2]
    place = own // n_grp
    w_in = attn_in.transpose(0, 2, 1, 3)
    bf = jnp.bfloat16
    dims = (n_rep, n_grp, n_img, rows, width)
    vm = lambda *s: pltpu.VMEM(s, bf)
    sem = lambda *s: pltpu.SemaphoreType.DMA(s)
    return pl.pallas_call(
        functools.partial(fused, dims),
        out_shape=jax.ShapeDtypeStruct((1, rows, recon_w), bf),
        in_specs=[pl.BlockSpec(memory_space=pl.ANY)] * 9,
        out_specs=pl.BlockSpec(memory_space=pltpu.VMEM),
        scratch_shapes=[
            vm(rows, p_size), vm(p_size, share), vm(loc_count, share), vm(width, recon_w),
            vm(n_grp, 3, depth, heads_w), vm(n_grp, 3, depth, heads_w),
            vm(n_grp, heads_w, depth), vm(n_grp, heads_w, depth),
            vm(n_grp, depth, hidden), vm(n_grp, hidden, depth),
            vm(n_img, rows, share), vm(rows, width), vm(n_img, own, width), vm(n_img, own, width),
            vm(3, rows, width), vm(3, n_img, own, width), vm(2, own, width),
            vm(n_grp, place, width), vm(n_grp, place, width), vm(n_img, n_grp, place, width),
            vm(rows, hidden),
            sem(sum(SPLIT), n_grp + 1), sem(sum(SPLIT), n_grp), sem(sum(SPLIT), n_grp), sem(sum(SPLIT), n_grp),
            sem(7, n_img, 2), sem(7, n_img, 2), sem(2, n_grp), sem(2, n_grp),
            sem(10),
        ],
        compiler_params=pltpu.CompilerParams(
            collective_id=0, has_side_effects=True, vmem_limit_bytes=60 * 1024 * 1024
        ),
    )(patches, embed_kernel, location_embed, w_in[0], w_in[1], attn_out, ffn_up, ffn_down, head_kernel)


def fits(mesh, rows):
    return mesh.shape["rep"] == 2 and mesh.shape["grp"] == 4 and mesh.shape["img"] == 4 and rows % (mesh.shape["grp"] * mesh.shape["img"] * 16) == 0


def serve(mesh, patches, *weights):
    loc_count = weights[1].shape[0]
    rows = patches.shape[1]
    if fits(mesh, rows) and rows // loc_count == mesh.shape["img"]:
        return local_fused(mesh, patches, *weights)
    return local(patches, *weights)


def solution(mesh):
    return jax.shard_map(
        functools.partial(serve, mesh),
        mesh=mesh,
        in_specs=(
            P("grp", "rep", None),
            P("grp", None, "img"),
            P(None, "img"),
            P(None, "grp", None, "img"),
            P(None, "img", "grp"),
            P("grp", "img"),
            P("img", "grp"),
            P("grp", None, "img"),
        ),
        out_specs=P("grp", "rep", "img"),
        check_vma=False,
    )
```
